128 devices in a mesh: dp: 16 (over x, z_lo, core), mp: 8 (over z_hi, y).
Axes of the slice: x: 4, y: 4, z: 4 (z_hi: 2, z_lo: 2; z = z_hi * 2 + z_lo), core: 2. Of those that a mesh axis runs over, the one named last changes fastest.
Arguments:
- inputs: bfloat16 [4096, 6144], P('dp', 'mp'), may hold values from -26 to 26
- out_grad: bfloat16 [4096, 6144], P('dp', 'mp'), may hold values from -6 to 6
- attn_grad: bfloat16 [4096, 6144], P('dp', 'mp'), may hold values from -6 to 6
- hidden_grad: bfloat16 [4096, 12288], P('dp', 'mp'), may hold values from -6 to 6
- gain: float32 [6144], replicated, may hold values from 0.1 to 1.9
- w_in: bfloat16 [6144, 12288], P(None, 'mp'), may hold values from -0.078125 to 0.078125
Outputs:
- input_grad: bfloat16 [4096, 6144], P('dp', 'mp')
- weight_grad: float32 [6144, 12288], P('dp', 'mp')
- gain_grad: float32 [6144], P('mp')
The draws below stay inside these ranges and needn't reach their ends.
All inputs are finite; a program needn't handle non-finite values.
Results may differ from the reference program's by a relative error of at most 0.02.
Values may be sent and summed in bfloat16 or wider, within the bound.
No kernel may reach another device: no remote copies, remote signals or barrier semaphores. Data moves between devices by JAX's collectives and lax.ppermute only.
A program may use at most 128 MiB of HBM per device.

```python
import math
import jax
import jax.numpy as jnp
from jax import lax

D = 6144
FF = 12288
TOK_DEV = 256
TOKENS = 4096
N_DP = 16
N_MP = 8


def draw_inputs(key, part):
    key = jax.random.fold_in(key, 11)
    key_base, key_rows = jax.random.split(key, 2)
    row_scales = jnp.exp(jax.random.uniform(key_rows, (TOKENS, 1), jnp.float32, math.log(0.2), math.log(2.0)))
    column_scales = 10.0 ** (jnp.arange(D, dtype=jnp.float32) / D - 0.5)
    base_values = jnp.clip(jax.random.normal(key_base, (TOKENS, D), jnp.float32), -4.0, 4.0)
    drawn = base_values * column_scales[None, :] * row_scales
    return drawn.astype(jnp.bfloat16)


def shard_levels(rng, shape, shards, low, high):
    level, own = 1.0, jax.random.fold_in(rng, 6)
    for dim, blocks in shards:
        heights = jnp.exp(jax.random.uniform(jax.random.fold_in(own, dim), (blocks,), jnp.float32, low / len(shards), high / len(shards)))
        level = level * jnp.repeat(heights, shape[dim] // blocks).reshape([-1 if axis == dim else 1 for axis in range(len(shape))])
    return level


def gaussian(stream_key, dims, width, limit, cuts=(), kind=jnp.bfloat16):
    array = width * jax.random.normal(stream_key, dims, jnp.float32)
    if cuts:
        array = array * shard_levels(stream_key, dims, cuts, -0.22, 0.18)
    return jnp.clip(array, -limit, limit).astype(kind)


def setup_inputs(seed: int = 0) -> dict:
    key_list = jax.random.split(jax.random.key(seed), 7)
    inputs = draw_inputs(jax.random.fold_in(key_list[6], 71), 0)
    out_grad = gaussian(key_list[1], (TOKENS, D), 1.0, 6.0, ((0, 16), (1, 8)))
    attn_grad = gaussian(key_list[2], (TOKENS, D), 1.0, 6.0, ((0, 16), (1, 8)))
    hidden_grad = gaussian(key_list[3], (TOKENS, FF), 1.0, 6.0, ((0, 16), (1, 8)))
    gain = jnp.clip(1.0 + 0.18 * jax.random.normal(key_list[4], (D,), jnp.float32), 0.1, 1.9)
    w_in = gaussian(key_list[5], (D, FF), D ** -0.5, 0.078125, ((1, 8),))
    return dict(inputs=inputs, out_grad=out_grad, attn_grad=attn_grad, hidden_grad=hidden_grad, gain=gain, w_in=w_in)


epsilon = 1e-06

def gelu_slope(values):
    normal_cdf = 0.5 * (1.0 + lax.erf(values * 0.7071067811865476))
    normal_pdf = jnp.exp(-0.5 * values * values) * 0.3989422804014327
    return normal_cdf + values * normal_pdf

def reference(inputs, out_grad, attn_grad, hidden_grad, gain, w_in):
    floated = inputs.astype(jnp.float32)
    centred = floated - lax.optimization_barrier(jnp.mean(floated, axis=1, keepdims=True))
    inv_scale = lax.rsqrt(lax.optimization_barrier(jnp.mean(centred * centred, axis=1, keepdims=True)) + epsilon)
    scaled = centred * inv_scale
    gain_full = gain.astype(jnp.float32)
    normed = (scaled * gain_full).astype(jnp.bfloat16)
    pre_act = jnp.dot(normed, w_in, preferred_element_type=jnp.float32)
    pre_grad = (hidden_grad.astype(jnp.float32) * gelu_slope(pre_act)).astype(jnp.bfloat16)

    def group_step(group_index, running):
        begin = (group_index * TOK_DEV).astype(jnp.int32)
        left_rows = lax.dynamic_slice_in_dim(normed, begin, TOK_DEV, 0)
        right_rows = lax.dynamic_slice_in_dim(pre_grad, begin, TOK_DEV, 0)
        partial_sum = lax.dot_general(left_rows, right_rows, (((0,), (0,)), ((), ())), preferred_element_type=jnp.float32)
        rounded = lax.optimization_barrier(partial_sum.astype(jnp.bfloat16))
        return running + rounded.astype(jnp.float32)
    weight_grad = lax.fori_loop(0, N_DP, group_step, jnp.zeros((D, FF), jnp.float32))
    block_width = FF // N_MP

    def block_step(block_index, running):
        begin = (block_index * block_width).astype(jnp.int32)
        grad_block = lax.dynamic_slice_in_dim(pre_grad, begin, block_width, 1)
        weight_block = lax.dynamic_slice_in_dim(w_in, begin, block_width, 1)
        partial_sum = lax.dot_general(grad_block, weight_block, (((1,), (1,)), ((), ())), preferred_element_type=jnp.float32)
        rounded = lax.optimization_barrier(partial_sum.astype(jnp.bfloat16))
        return running + rounded.astype(jnp.float32)
    summed = lax.fori_loop(0, N_MP, block_step, jnp.zeros((TOKENS, D), jnp.float32))
    dnorm = summed + attn_grad.astype(jnp.float32)
    dxhat = dnorm * gain_full
    first_mean = lax.optimization_barrier(jnp.mean(dxhat, axis=1, keepdims=True))
    second_mean = lax.optimization_barrier(jnp.mean(dxhat * scaled, axis=1, keepdims=True))
    input_grad = (out_grad.astype(jnp.float32) + inv_scale * (dxhat - first_mean - scaled * second_mean)).astype(jnp.bfloat16)
    gain_grad = lax.optimization_barrier(jnp.sum(dnorm * scaled, axis=0))
    return (input_grad, weight_grad, gain_grad)
```

```python
import jax
import jax.numpy as jnp
from jax import lax
from jax.sharding import Mesh, PartitionSpec as P

epsilon = 1e-06
DP = ("x", "zl", "c")
MP = ("zh", "y")
f32 = jnp.float32
bf16 = jnp.bfloat16


def gelu_slope(values):
    normal_cdf = 0.5 * (1.0 + lax.erf(values * 0.7071067811865476))
    normal_pdf = jnp.exp(-0.5 * values * values) * 0.3989422804014327
    return normal_cdf + values * normal_pdf


def shift(value, axis, step, size):
    return lax.ppermute(value, axis, [(i, (i + step) % size) for i in range(size)])


def columns(value, index, width):
    return lax.dynamic_slice_in_dim(value, index * width, width, 1)


def local(inputs, out_grad, attn_grad, hidden_grad, gain, w_in):
    own = inputs.shape[1]
    x, zl, c = (lax.axis_index(name) for name in DP)
    zh, y = (lax.axis_index(name) for name in MP)

    def block(dz, dy):
        return (zh ^ dz) * 4 + (y + dy) % 4

    parts = {(0, 0): inputs}
    parts[1, 0] = shift(inputs, "zh", 1, 2)
    parts[0, 3] = shift(inputs, "y", 1, 4)
    parts[0, 1] = shift(inputs, "y", 3, 4)
    parts[0, 2] = shift(inputs, "y", 2, 4)
    parts[1, 3] = shift(parts[1, 0], "y", 1, 4)
    parts[1, 1] = shift(parts[1, 0], "y", 3, 4)
    parts[1, 2] = shift(parts[0, 2], "zh", 1, 2)
    gathered = jnp.zeros((inputs.shape[0], own * 8), bf16)
    for (dz, dy), part in parts.items():
        gathered = lax.dynamic_update_slice_in_dim(gathered, part, block(dz, dy) * own, 1)
    floated = gathered.astype(f32)
    mean = jnp.mean(floated, axis=1, keepdims=True)
    centred = floated - mean
    inv_scale = lax.rsqrt(jnp.mean(centred * centred, axis=1, keepdims=True) + epsilon)
    scaled = centred * inv_scale
    normed = (scaled * gain).astype(bf16)

    wide = 2 * own
    normed_x = [columns(normed, x, wide)]
    for step in (1, 2, 3):
        normed_x.append(shift(columns(normed, (x + step) % 4, wide), "x", step, 4))

    pre_act = jnp.dot(normed, w_in, preferred_element_type=f32)
    pre_grad = (hidden_grad.astype(f32) * gelu_slope(pre_act)).astype(bf16)

    grads_x = [pre_grad] + [shift(pre_grad, "x", step, 4) for step in (1, 2, 3)]

    term = lax.dot_general(pre_grad, w_in, (((1,), (1,)), ((), ())), preferred_element_type=f32).astype(bf16)

    def piece(dz, dy):
        return columns(term, block(dz, dy), own)

    got_z = shift(piece(1, 2), "zh", 1, 2)
    got_p = shift(piece(1, 1), "y", 1, 4)
    got_m = shift(piece(1, 3), "y", 3, 4)
    near_p = shift(piece(0, 1), "y", 1, 4)
    near_m = shift(piece(0, 3), "y", 3, 4)
    far = shift((piece(0, 2).astype(f32) + got_z.astype(f32)).astype(bf16), "y", 2, 4)
    across = shift(
        (piece(1, 0).astype(f32) + got_p.astype(f32) + got_m.astype(f32)).astype(bf16), "zh", 1, 2
    )

    scaled_own = columns(scaled, block(0, 0), own)
    gain_own = lax.dynamic_slice_in_dim(gain, block(0, 0) * own, own, 0)
    attn = attn_grad.astype(f32)
    weighted = term.astype(f32) * gain
    sums = jnp.stack(
        [
            jnp.sum(weighted, axis=1) + jnp.sum(attn * gain_own, axis=1),
            jnp.sum(weighted * scaled, axis=1) + jnp.sum(attn * gain_own * scaled_own, axis=1),
        ]
    )
    sums = sums + shift(sums, "y", 1, 4) + shift(sums, "y", 2, 4) + shift(sums, "y", 3, 4)
    sums = (sums + shift(sums, "zh", 1, 2)) * (1.0 / (own * 8))
    first_mean, second_mean = sums[0][:, None], sums[1][:, None]

    normed_all = jnp.concatenate(normed_x, 0)
    grads_all = jnp.concatenate(grads_x, 0)
    rows = wide // 4

    def weight_part(dzl, dc):
        left = columns(normed_all, (zl ^ dzl) * 2 + (c ^ dc), rows)
        return lax.dot_general(left, grads_all, (((0,), (0,)), ((), ())), preferred_element_type=f32)

    sent = shift(weight_part(1, 1).astype(bf16), "c", 1, 2)
    sent = shift((weight_part(1, 0) + sent.astype(f32)).astype(bf16), "zl", 1, 2)
    other = shift(weight_part(0, 1).astype(bf16), "c", 1, 2)
    weight_grad = weight_part(0, 0) + other.astype(f32) + sent.astype(f32)

    dnorm = attn + piece(0, 0).astype(f32)
    for got in (near_p, near_m, far, across):
        dnorm = dnorm + got.astype(f32)
    dxhat = dnorm * gain_own
    input_grad = (
        out_grad.astype(f32) + inv_scale * (dxhat - first_mean - scaled_own * second_mean)
    ).astype(bf16)
    gain_grad = jnp.sum(dnorm * scaled_own, axis=0)
    gain_grad = gain_grad + shift(gain_grad, "c", 1, 2)
    gain_grad = gain_grad + shift(gain_grad, "zl", 1, 2)
    gain_grad = (
        gain_grad + shift(gain_grad, "x", 1, 4) + shift(gain_grad, "x", 2, 4) + shift(gain_grad, "x", 3, 4)
    )
    return (input_grad, weight_grad, gain_grad)


def solution(mesh):
    fine = Mesh(mesh.devices.reshape(4, 2, 2, 2, 4), DP + MP)
    both = P(DP, MP)
    in_specs = (both, both, both, both, P(), P(None, MP))
    out_specs = (both, both, P(MP))
    return jax.shard_map(local, mesh=fine, in_specs=in_specs, out_specs=out_specs, check_vma=False)
```

```python
import functools
import jax
import jax.numpy as jnp
from jax import lax
from jax.experimental import pallas as pl
from jax.experimental.pallas import tpu as pltpu
from jax.sharding import Mesh, PartitionSpec as P

epsilon = 1e-06
DP = ("x", "zl", "c")
MP = ("zh", "y")
f32 = jnp.float32
bf16 = jnp.bfloat16


def gelu_slope(values):
    normal_cdf = 0.5 * (1.0 + lax.erf(values * 0.7071067811865476))
    normal_pdf = jnp.exp(-0.5 * values * values) * 0.3989422804014327
    return normal_cdf + values * normal_pdf


def shift(value, axis, step, size):
    return lax.ppermute(value, axis, [(i, (i + step) % size) for i in range(size)])


def after(value, *done):
    return lax.optimization_barrier((value, *done))[0]


def in_hbm(value):
    return pltpu.with_memory_space_constraint(value, pltpu.HBM)


def call(kernel, grid, in_specs, out_specs, out_shape, scratch, name, mib, flops, moved):
    step = pl.pallas_call(
        kernel,
        grid_spec=pltpu.PrefetchScalarGridSpec(
            num_scalar_prefetch=1, grid=grid, in_specs=in_specs, out_specs=out_specs, scratch_shapes=scratch
        ),
        out_shape=[pltpu.HBM(s.shape, s.dtype) for s in out_shape],
        compiler_params=pltpu.CompilerParams(vmem_limit_bytes=mib * 2**20),
        cost_estimate=pl.CostEstimate(flops=flops, bytes_accessed=moved, transcendentals=0),
        name=name,
    )
    return lambda ids, *operands: step(ids, *map(in_hbm, operands))
    return lambda ids, *operands: step(ids, *map(in_hbm, operands))


def whole(shape):
    return pl.BlockSpec(shape, lambda i, ids: (0,) * len(shape))


def along(ref, block, width):
    return ref[:, pl.ds(pl.multiple_of(block * width, 128), width)]


def normalise(parts, ids, wanted, gain, strip):
    n, (rows, own) = len(parts), parts[0].shape
    m = len(wanted)

    def kernel(ids_ref, *refs):
        part_refs, (gain_ref, *refs) = refs[:n], refs[n:]
        normed_ref, mean_ref, inv_ref, *out_refs = refs
        total = sum(jnp.sum(r[...].astype(f32), axis=1, keepdims=True) for r in part_refs)
        mean = total * (1.0 / (n * own))
        square = sum(jnp.sum(jnp.square(r[...].astype(f32) - mean), axis=1, keepdims=True) for r in part_refs)
        inv = lax.rsqrt(square * (1.0 / (n * own)) + epsilon)
        mean_ref[...] = jnp.broadcast_to(mean, (strip, 128))
        inv_ref[...] = jnp.broadcast_to(inv, (strip, 128))
        for k in range(n):
            scaled = (part_refs[k][...].astype(f32) - mean) * inv
            normed = (scaled * along(gain_ref, ids_ref[k], own)).astype(bf16)
            normed_ref[:, pl.ds(pl.multiple_of(ids_ref[k] * own, 128), own)] = normed
        for k in range(m):
            out_refs[k][...] = along(normed_ref, ids_ref[n + k], own)

    def strips(width):
        return pl.BlockSpec((strip, width), lambda i, ids: (i, 0))

    return call(
        kernel,
        (rows // strip,),
        [strips(own)] * n + [whole(gain.shape)],
        [strips(n * own)] + [strips(128)] * 2 + [strips(own)] * m,
        [jax.ShapeDtypeStruct((rows, n * own), bf16)]
        + [jax.ShapeDtypeStruct((rows, 128), f32)] * 2
        + [jax.ShapeDtypeStruct((rows, own), bf16)] * m,
        [],
        "normalise",
        10,
        0,
        10 * n * rows * own,
    )(jnp.stack(ids + wanted), *parts, gain)


def project(normed, w_in, hidden, step):
    rows, width = hidden.shape
    strips = [slice(k * step, (k + 1) * step) for k in range(width // step)]

    def kernel(normed_ref, w_ref, hidden_ref, out_ref, w, done):
        copies = [
            pltpu.make_async_copy(w_ref.at[:, strip], w.at[:, strip], done.at[k]) for k, strip in enumerate(strips)
        ]
        for copy in copies:
            copy.start()
        for copy, strip in zip(copies, strips):
            copy.wait()
            pre = jnp.dot(normed_ref[...], w[:, strip], preferred_element_type=f32)
            out_ref[:, strip] = (hidden_ref[:, strip].astype(f32) * gelu_slope(pre)).astype(bf16)

    return pl.pallas_call(
        kernel,
        grid=(1,),
        in_specs=[
            pl.BlockSpec(normed.shape, lambda j: (0, 0)),
            pl.BlockSpec(memory_space=pl.ANY),
            pl.BlockSpec((rows, width), lambda j: (0, 0)),
        ],
        out_specs=pl.BlockSpec((rows, width), lambda j: (0, 0)),
        out_shape=jax.ShapeDtypeStruct((rows, width), bf16),
        scratch_shapes=[pltpu.VMEM(w_in.shape, bf16), pltpu.SemaphoreType.DMA((len(strips),))],
        compiler_params=pltpu.CompilerParams(vmem_limit_bytes=32 * 2**20),
        cost_estimate=pl.CostEstimate(flops=2 * normed.size * width, bytes_accessed=2 * w_in.size, transcendentals=hidden.size),
        name="project",
    )(normed, in_hbm(w_in), hidden)


def spread(pre_grad, ids, w_in, own, ahead):
    n, (rows, depth) = len(ids), pre_grad.shape

    def kernel(ids_ref, grad_ref, w_ref, *refs):
        out_refs, (blocks, done) = refs[:n], refs[n:]
        copies = [
            pltpu.make_async_copy(
                w_ref.at[pl.ds(pl.multiple_of(ids_ref[k] * own, own), own), :],
                blocks.at[k % ahead],
                done.at[k % ahead],
            )
            for k in range(n)
        ]
        for k in range(ahead):
            copies[k].start()
        for k in range(n):
            copies[k].wait()
            out_refs[k][...] = lax.dot_general(
                grad_ref[...], blocks[k % ahead], (((1,), (1,)), ((), ())), preferred_element_type=f32
            ).astype(bf16)
            if k + ahead < n:
                copies[k + ahead].start()

    return call(
        kernel,
        (1,),
        [whole((rows, depth)), pl.BlockSpec(memory_space=pl.ANY)],
        [whole((rows, own))] * n,
        [jax.ShapeDtypeStruct((rows, own), bf16)] * n,
        [pltpu.VMEM((ahead, own, depth), bf16), pltpu.SemaphoreType.DMA((ahead,))],
        "spread",
        20,
        2 * n * rows * own * depth,
        2 * w_in.size,
    )(jnp.stack(ids), pre_grad, w_in)


def outer(same, crossed, grads, half, width, sides, cores, rows):
    tokens = same[0].shape[0]
    cut = tokens // 2
    terms = [
        [(0, 0, 0, tokens), (1, 0, 1, tokens), (2, 0, 2, tokens), (3, 0, 3, cut), (3, cut, 4, cut)],
        [(0, 0, 0, tokens), (1, 0, 1, tokens), (1, tokens, 3, cut), (2, 0, 2, tokens), (2, tokens, 4, cut)],
    ]

    def kernel(ids_ref, *refs):
        same_refs, crossed_refs, grads_refs, (sent_ref, kept_ref) = refs[:4], refs[4:7], refs[7:12], refs[12:]
        i = pl.program_id(0)
        for side, left_refs in enumerate((same_refs, crossed_refs)):

            @pl.when(ids_ref[i] == side)
            def _():
                column = pl.ds(pl.multiple_of(ids_ref[4 + i] * rows, 128), rows)
                total = None
                for k, at, group, size in terms[side]:
                    term = lax.dot_general(
                        left_refs[k][at : at + size, column],
                        grads_refs[group][...],
                        (((0,), (0,)), ((), ())),
                        preferred_element_type=f32,
                    )
                    total = term if total is None else total + term

                @pl.when(i < 2)
                def _():
                    sent_ref[...] = total.astype(bf16)

                @pl.when(i >= 2)
                def _():
                    kept_ref[...] = total

    return call(
        kernel,
        (4,),
        [whole(p.shape) for p in (*same, *crossed)]
        + [pl.BlockSpec((g.shape[0], width), lambda i, ids: (0, half)) for g in grads],
        [
            pl.BlockSpec((rows, width), lambda i, ids: (jnp.minimum(i, 1), 0)),
            pl.BlockSpec((rows, width), lambda i, ids: (jnp.maximum(i - 2, 0), 0)),
        ],
        [jax.ShapeDtypeStruct((2 * rows, width), bf16), jax.ShapeDtypeStruct((2 * rows, width), f32)],
        [],
        "outer",
        16,
        32 * rows * tokens * width,
        32 * tokens * width,
    )(jnp.stack(sides + cores), *same, *crossed, *grads)


def local(inputs, out_grad, attn_grad, hidden_grad, gain, w_in):
    tokens, own = inputs.shape
    hidden = w_in.shape[1]
    x, zl, c = (lax.axis_index(name) for name in DP)
    zh, y = (lax.axis_index(name) for name in MP)
    gain_row = gain[None, :]
    parity = y % 2
    cut = tokens // 2

    def block(dz, dy):
        return (zh ^ dz) * 4 + (y + dy) % 4

    parts = {(0, 0): inputs}
    parts[1, 0] = shift(inputs, "zh", 1, 2)
    parts[0, 2] = shift(inputs, "y", 2, 4)
    parts[0, 3] = shift(inputs, "y", 1, 4)
    parts[0, 1] = shift(inputs, "y", 3, 4)
    parts[1, 2] = shift(parts[0, 2], "zh", 1, 2)
    parts[1, 3] = shift(parts[1, 0], "y", 1, 4)
    parts[1, 1] = shift(parts[1, 0], "y", 3, 4)
    keys = list(parts)
    wanted = [2 * ((x + step) % 4) + parity for step in range(4)] + [2 * x + 1 - parity]
    normed, mean, inv, *sends, crossed_own = normalise(
        [parts[k] for k in keys], [block(*k) for k in keys], wanted, gain_row, 64
    )

    same = [sends[0], shift(sends[1], "x", 1, 4), shift(sends[3], "x", 3, 4), shift(sends[2], "x", 2, 4)]

    pre_grad = project(normed, w_in, hidden_grad, 512)

    low, high = shift(pre_grad, "x", 1, 4), shift(pre_grad, "x", 3, 4)

    same[3] = after(same[3], pre_grad)
    down = shift(jnp.concatenate([same[1], same[3][:cut]], 0), "y", 3, 4)
    up = shift(jnp.concatenate([same[2], same[3][cut:]], 0), "y", 1, 4)
    crossed = [crossed_own, down, up]

    pieces = dict(zip(keys, spread(pre_grad, [block(*k) for k in keys], w_in, own, 4)))
    got_z = shift(pieces[1, 2], "zh", 1, 2)
    got_p = shift(after(pieces[1, 1], down, up), "y", 1, 4)
    got_m = shift(after(pieces[1, 3], down, up), "y", 3, 4)
    near_p = shift(after(pieces[0, 1], got_p, got_m), "y", 1, 4)
    near_m = shift(after(pieces[0, 3], got_p, got_m), "y", 3, 4)
    far = shift((pieces[0, 2].astype(f32) + got_z.astype(f32)).astype(bf16), "y", 2, 4)
    across = shift((pieces[1, 0].astype(f32) + got_p.astype(f32) + got_m.astype(f32)).astype(bf16), "zh", 1, 2)

    far_low = shift(after(low[:cut], pieces[0, 0]), "x", 1, 4)
    far_high = shift(after(high[cut:], pieces[0, 0]), "x", 3, 4)
    grads = [pre_grad, low, high, far_low, far_high]

    rows = own // 2
    sides = [zl ^ 1 ^ parity, zl ^ parity] * 2
    cores = [1 - c, 1 - c, c, c]
    weight_parts = []
    got = None
    for half in (0, 1):
        sent, kept = outer(same, crossed, grads, half, hidden // 2, sides, cores, rows)
        got_c = shift(sent, "c", 1, 2)
        if got is not None:
            got_c = after(got_c, got)
        got = shift((kept[:rows] + got_c[:rows].astype(f32)).astype(bf16), "zl", 1, 2)
        weight_parts.append((kept[rows:] + got_c[rows:].astype(f32)) + got.astype(f32))
    weight_grad = jnp.concatenate(weight_parts, 1)

    mean, inv = mean[:, :1], inv[:, :1]
    scaled_own = (inputs.astype(f32) - mean) * inv
    gain_own = lax.dynamic_slice_in_dim(gain, block(0, 0) * own, own, 0)
    dnorm = attn_grad.astype(f32) + pieces[0, 0].astype(f32)
    for value in (near_p, near_m, far, across):
        dnorm = dnorm + value.astype(f32)
    dxhat = dnorm * gain_own
    sums = jnp.stack([jnp.sum(dxhat, axis=1), jnp.sum(dxhat * scaled_own, axis=1)])
    for axis, step, size in (("zh", 1, 2), ("y", 2, 4), ("y", 1, 4)):
        sums = sums + shift(sums, axis, step, size)
    sums = sums * (1.0 / (own * 8))
    first_mean, second_mean = sums[0][:, None], sums[1][:, None]
    input_grad = (out_grad.astype(f32) + inv * (dxhat - first_mean - scaled_own * second_mean)).astype(bf16)
    gain_grad = jnp.sum(dnorm * scaled_own, axis=0)
    for axis, step, size in (("c", 1, 2), ("zl", 1, 2), ("x", 2, 4), ("x", 1, 4)):
        gain_grad = gain_grad + shift(gain_grad, axis, step, size)
    return (input_grad, weight_grad, gain_grad)


def solution(mesh):
    fine = Mesh(mesh.devices.reshape(4, 2, 2, 2, 4), DP + MP)
    both = P(DP, MP)
    in_specs = (both, both, both, both, P(), P(None, MP))
    out_specs = (both, both, P(MP))
    return jax.shard_map(local, mesh=fine, in_specs=in_specs, out_specs=out_specs, check_vma=False)
```

```python
import functools
import jax
import jax.numpy as jnp
from jax import lax
from jax.experimental import pallas as pl
from jax.experimental.pallas import tpu as pltpu
from jax.sharding import Mesh, PartitionSpec as P

epsilon = 1e-06
DP = ("x", "zl", "c")
MP = ("zh", "y")
f32 = jnp.float32
bf16 = jnp.bfloat16


def gelu_slope(values):
    normal_cdf = 0.5 * (1.0 + lax.erf(values * 0.7071067811865476))
    normal_pdf = jnp.exp(-0.5 * values * values) * 0.3989422804014327
    return normal_cdf + values * normal_pdf


def shift(value, axis, step, size):
    return lax.ppermute(value, axis, [(i, (i + step) % size) for i in range(size)])


def after(value, *done):
    return lax.optimization_barrier((value, *done))[0]


def in_hbm(value):
    return pltpu.with_memory_space_constraint(value, pltpu.HBM)


def call(kernel, grid, in_specs, out_specs, out_shape, scratch, name, mib, flops, moved, free=0):
    step = pl.pallas_call(
        kernel,
        grid_spec=pltpu.PrefetchScalarGridSpec(
            num_scalar_prefetch=1, grid=grid, in_specs=in_specs, out_specs=out_specs, scratch_shapes=scratch
        ),
        out_shape=[pltpu.HBM(s.shape, s.dtype) if k >= free else s for k, s in enumerate(out_shape)],
        compiler_params=pltpu.CompilerParams(vmem_limit_bytes=mib * 2**20),
        cost_estimate=pl.CostEstimate(flops=flops, bytes_accessed=moved, transcendentals=0),
        name=name,
    )
    return lambda ids, *operands: step(ids, *map(in_hbm, operands))
    return lambda ids, *operands: step(ids, *map(in_hbm, operands))


def whole(shape):
    return pl.BlockSpec(shape, lambda i, ids: (0,) * len(shape))


def along(ref, block, width):
    return ref[:, pl.ds(pl.multiple_of(block * width, 128), width)]


def normalise(parts, ids, wanted, gain, strip):
    n, (rows, own) = len(parts), parts[0].shape
    m = len(wanted)

    def kernel(ids_ref, *refs):
        part_refs, (gain_ref, *refs) = refs[:n], refs[n:]
        normed_ref, mean_ref, inv_ref, *out_refs = refs
        total = sum(jnp.sum(r[...].astype(f32), axis=1, keepdims=True) for r in part_refs)
        mean = total * (1.0 / (n * own))
        square = sum(jnp.sum(jnp.square(r[...].astype(f32) - mean), axis=1, keepdims=True) for r in part_refs)
        inv = lax.rsqrt(square * (1.0 / (n * own)) + epsilon)
        mean_ref[...] = jnp.broadcast_to(mean, (strip, 128))
        inv_ref[...] = jnp.broadcast_to(inv, (strip, 128))
        for k in range(n):
            scaled = (part_refs[k][...].astype(f32) - mean) * inv
            normed = (scaled * along(gain_ref, ids_ref[k], own)).astype(bf16)
            normed_ref[:, pl.ds(pl.multiple_of(ids_ref[k] * own, 128), own)] = normed
        for k in range(m):
            out_refs[k][...] = along(normed_ref, ids_ref[n + k], own)

    def strips(width):
        return pl.BlockSpec((strip, width), lambda i, ids: (i, 0))

    return call(
        kernel,
        (rows // strip,),
        [strips(own)] * n + [whole(gain.shape)],
        [strips(n * own)] + [strips(128)] * 2 + [strips(own)] * m,
        [jax.ShapeDtypeStruct((rows, n * own), bf16)]
        + [jax.ShapeDtypeStruct((rows, 128), f32)] * 2
        + [jax.ShapeDtypeStruct((rows, own), bf16)] * m,
        [],
        "normalise",
        10,
        0,
        10 * n * rows * own,
        1,
    )(jnp.stack(ids + wanted), *parts, gain)


def project(normed, w_in, hidden, step):
    rows, width = hidden.shape
    strips = [slice(k * step, (k + 1) * step) for k in range(width // step)]

    def kernel(normed_ref, w_ref, hidden_ref, out_ref, w, done):
        copies = [
            pltpu.make_async_copy(w_ref.at[:, strip], w.at[:, strip], done.at[k]) for k, strip in enumerate(strips)
        ]
        for copy in copies:
            copy.start()
        for copy, strip in zip(copies, strips):
            copy.wait()
            pre = jnp.dot(normed_ref[...], w[:, strip], preferred_element_type=f32)
            out_ref[:, strip] = (hidden_ref[:, strip].astype(f32) * gelu_slope(pre)).astype(bf16)

    return pl.pallas_call(
        kernel,
        grid=(1,),
        in_specs=[
            pl.BlockSpec(normed.shape, lambda j: (0, 0)),
            pl.BlockSpec(memory_space=pl.ANY),
            pl.BlockSpec((rows, width), lambda j: (0, 0)),
        ],
        out_specs=pl.BlockSpec((rows, width), lambda j: (0, 0)),
        out_shape=jax.ShapeDtypeStruct((rows, width), bf16),
        scratch_shapes=[pltpu.VMEM(w_in.shape, bf16), pltpu.SemaphoreType.DMA((len(strips),))],
        compiler_params=pltpu.CompilerParams(vmem_limit_bytes=32 * 2**20),
        cost_estimate=pl.CostEstimate(flops=2 * normed.size * width, bytes_accessed=2 * w_in.size, transcendentals=hidden.size),
        name="project",
    )(normed, in_hbm(w_in), hidden)


def spread(pre_grad, ids, w_in, own, ahead):
    n, (rows, depth) = len(ids), pre_grad.shape

    def kernel(ids_ref, grad_ref, w_ref, *refs):
        out_refs, (blocks, done) = refs[:n], refs[n:]
        copies = [
            pltpu.make_async_copy(
                w_ref.at[pl.ds(pl.multiple_of(ids_ref[k] * own, own), own), :],
                blocks.at[k % ahead],
                done.at[k % ahead],
            )
            for k in range(n)
        ]
        for k in range(ahead):
            copies[k].start()
        for k in range(n):
            copies[k].wait()
            out_refs[k][...] = lax.dot_general(
                grad_ref[...], blocks[k % ahead], (((1,), (1,)), ((), ())), preferred_element_type=f32
            ).astype(bf16)
            if k + ahead < n:
                copies[k + ahead].start()

    return call(
        kernel,
        (1,),
        [whole((rows, depth)), pl.BlockSpec(memory_space=pl.ANY)],
        [whole((rows, own))] * n,
        [jax.ShapeDtypeStruct((rows, own), bf16)] * n,
        [pltpu.VMEM((ahead, own, depth), bf16), pltpu.SemaphoreType.DMA((ahead,))],
        "spread",
        20,
        2 * n * rows * own * depth,
        2 * w_in.size,
    )(jnp.stack(ids), pre_grad, w_in)


def outer(same, crossed, grads, half, width, sides, cores, rows):
    tokens = same[0].shape[0]
    cut = tokens // 2
    terms = [
        [(0, 0, 0, tokens), (1, 0, 1, tokens), (2, 0, 2, tokens), (3, 0, 3, cut), (3, cut, 4, cut)],
        [(0, 0, 0, tokens), (1, 0, 1, tokens), (1, tokens, 3, cut), (2, 0, 2, tokens), (2, tokens, 4, cut)],
    ]

    def kernel(ids_ref, *refs):
        same_refs, crossed_refs, grads_refs, (sent_ref, kept_ref) = refs[:4], refs[4:7], refs[7:12], refs[12:]
        i = pl.program_id(0)
        for side, left_refs in enumerate((same_refs, crossed_refs)):

            @pl.when(ids_ref[i] == side)
            def _():
                column = pl.ds(pl.multiple_of(ids_ref[4 + i] * rows, 128), rows)
                total = None
                for k, at, group, size in terms[side]:
                    term = lax.dot_general(
                        left_refs[k][at : at + size, column],
                        grads_refs[group][...],
                        (((0,), (0,)), ((), ())),
                        preferred_element_type=f32,
                    )
                    total = term if total is None else total + term

                @pl.when(i < 2)
                def _():
                    sent_ref[...] = total.astype(bf16)

                @pl.when(i >= 2)
                def _():
                    kept_ref[...] = total

    return call(
        kernel,
        (4,),
        [whole(p.shape) for p in (*same, *crossed)]
        + [pl.BlockSpec((g.shape[0], width), lambda i, ids: (0, half)) for g in grads],
        [
            pl.BlockSpec((rows, width), lambda i, ids: (jnp.minimum(i, 1), 0)),
            pl.BlockSpec((rows, width), lambda i, ids: (jnp.maximum(i - 2, 0), 0)),
        ],
        [jax.ShapeDtypeStruct((2 * rows, width), bf16), jax.ShapeDtypeStruct((2 * rows, width), f32)],
        [],
        "outer",
        16,
        32 * rows * tokens * width,
        32 * tokens * width,
    )(jnp.stack(sides + cores), *same, *crossed, *grads)


def local(inputs, out_grad, attn_grad, hidden_grad, gain, w_in):
    tokens, own = inputs.shape
    hidden = w_in.shape[1]
    x, zl, c = (lax.axis_index(name) for name in DP)
    zh, y = (lax.axis_index(name) for name in MP)
    gain_row = gain[None, :]
    parity = y % 2
    cut = tokens // 2

    def block(dz, dy):
        return (zh ^ dz) * 4 + (y + dy) % 4

    parts = {(0, 0): inputs}
    parts[1, 0] = shift(inputs, "zh", 1, 2)
    parts[0, 2] = shift(inputs, "y", 2, 4)
    parts[0, 3] = shift(inputs, "y", 1, 4)
    parts[0, 1] = shift(inputs, "y", 3, 4)
    parts[1, 2] = shift(parts[0, 2], "zh", 1, 2)
    parts[1, 3] = shift(parts[1, 0], "y", 1, 4)
    parts[1, 1] = shift(parts[1, 0], "y", 3, 4)
    keys = list(parts)
    wanted = [2 * ((x + step) % 4) + parity for step in range(4)] + [2 * x + 1 - parity]
    normed, mean, inv, *sends, crossed_own = normalise(
        [parts[k] for k in keys], [block(*k) for k in keys], wanted, gain_row, 64
    )

    same = [sends[0], shift(sends[1], "x", 1, 4), shift(sends[3], "x", 3, 4), shift(sends[2], "x", 2, 4)]

    pre_grad = project(normed, w_in, hidden_grad, 512)

    low, high = shift(pre_grad, "x", 1, 4), shift(pre_grad, "x", 3, 4)

    same[3] = after(same[3], pre_grad)
    down = shift(jnp.concatenate([same[1], same[3][:cut]], 0), "y", 3, 4)
    up = shift(jnp.concatenate([same[2], same[3][cut:]], 0), "y", 1, 4)
    crossed = [crossed_own, down, up]

    pieces = dict(zip(keys, spread(pre_grad, [block(*k) for k in keys], w_in, own, 4)))
    got_z = shift(pieces[1, 2], "zh", 1, 2)
    got_p = shift(after(pieces[1, 1], down, up), "y", 1, 4)
    got_m = shift(after(pieces[1, 3], down, up), "y", 3, 4)
    near_p = shift(after(pieces[0, 1], down, up), "y", 1, 4)
    near_m = shift(after(pieces[0, 3], down, up), "y", 3, 4)
    far_sent = (pieces[0, 2].astype(f32) + got_z.astype(f32)).astype(bf16)
    far = shift(far_sent, "y", 2, 4)
    across_sent = (pieces[1, 0].astype(f32) + got_p.astype(f32) + got_m.astype(f32)).astype(bf16)
    across = shift(across_sent, "zh", 1, 2)

    far_low = shift(after(low[:cut], pieces[0, 0]), "x", 1, 4)
    far_high = shift(after(high[cut:], pieces[0, 0]), "x", 3, 4)
    grads = [pre_grad, low, high, far_low, far_high]

    rows = own // 2
    sides = [zl ^ 1 ^ parity, zl ^ parity] * 2
    cores = [1 - c, 1 - c, c, c]
    def pair(value, axis, step, size):
        return value + shift(value, axis, step, size)

    def send_late(kept, got_c):
        late = (kept[:rows] + got_c[:rows].astype(f32)).astype(bf16)
        return late, shift(late, "zl", 1, 2)

    width = hidden // 2
    sent_a, kept_a = outer(same, crossed, [after(pre_grad, far_sent)] + grads[1:], 0, width, sides, cores, rows)
    got_ca = shift(after(sent_a, got_p, got_m), "c", 1, 2)
    ready = after(pre_grad, sent_a)
    sent_b, kept_b = outer(same, crossed, [ready] + grads[1:], 1, width, sides, cores, rows)
    late, got_a = send_late(kept_a, after(got_ca, across, sent_b))
    got_cb = shift(sent_b, "c", 1, 2)
    late, got_b = send_late(kept_b, after(got_cb, got_a))
    weight_a = kept_a[rows:] + got_ca[rows:].astype(f32) + got_a.astype(f32)
    weight_b = kept_b[rows:] + got_cb[rows:].astype(f32) + got_b.astype(f32)
    weight_grad = jnp.concatenate([weight_a, weight_b], 1)

    mean, inv = mean[:, :1], inv[:, :1]
    scaled_own = (inputs.astype(f32) - mean) * inv
    gain_own = lax.dynamic_slice_in_dim(gain, block(0, 0) * own, own, 0)
    dnorm = attn_grad.astype(f32) + pieces[0, 0].astype(f32)
    for value in (near_p, near_m, far, across):
        dnorm = dnorm + value.astype(f32)
    dxhat = dnorm * gain_own
    sums = jnp.stack([jnp.sum(dxhat, axis=1), jnp.sum(dxhat * scaled_own, axis=1)])
    gain_grad = jnp.sum(dnorm * scaled_own, axis=0)

    sums = pair(pair(sums, "y", 2, 4), "zh", 1, 2)
    gain_grad = pair(pair(pair(gain_grad, "c", 1, 2), "x", 2, 4), "zl", 1, 2)
    sums = pair(after(sums, late), "y", 1, 4) * (1.0 / (own * 8))
    gain_grad = pair(after(gain_grad, late), "x", 1, 4)
    first_mean, second_mean = sums[0][:, None], sums[1][:, None]
    input_grad = (out_grad.astype(f32) + inv * (dxhat - first_mean - scaled_own * second_mean)).astype(bf16)
    return (input_grad, weight_grad, gain_grad)


def solution(mesh):
    fine = Mesh(mesh.devices.reshape(4, 2, 2, 2, 4), DP + MP)
    both = P(DP, MP)
    in_specs = (both, both, both, both, P(), P(None, MP))
    out_specs = (both, both, P(MP))
    return jax.shard_map(local, mesh=fine, in_specs=in_specs, out_specs=out_specs, check_vma=False)
```

```python
import functools
import jax
import jax.numpy as jnp
from jax import lax
from jax.experimental import pallas as pl
from jax.experimental.pallas import tpu as pltpu
from jax.sharding import Mesh, PartitionSpec as P

epsilon = 1e-06
DP = ("x", "zl", "c")
MP = ("zh", "y")
f32 = jnp.float32
bf16 = jnp.bfloat16


def gelu_slope(values):
    normal_cdf = 0.5 * (1.0 + lax.erf(values * 0.7071067811865476))
    normal_pdf = jnp.exp(-0.5 * values * values) * 0.3989422804014327
    return normal_cdf + values * normal_pdf


def shift(value, axis, step, size):
    return lax.ppermute(value, axis, [(i, (i + step) % size) for i in range(size)])


def after(value, *done):
    return lax.optimization_barrier((value, *done))[0]


def in_hbm(value):
    return pltpu.with_memory_space_constraint(value, pltpu.HBM)


def call(kernel, grid, in_specs, out_specs, out_shape, scratch, name, mib, flops, moved, free=0):
    step = pl.pallas_call(
        kernel,
        grid_spec=pltpu.PrefetchScalarGridSpec(
            num_scalar_prefetch=1, grid=grid, in_specs=in_specs, out_specs=out_specs, scratch_shapes=scratch
        ),
        out_shape=[pltpu.HBM(s.shape, s.dtype) if k >= free else s for k, s in enumerate(out_shape)],
        compiler_params=pltpu.CompilerParams(vmem_limit_bytes=mib * 2**20),
        cost_estimate=pl.CostEstimate(flops=flops, bytes_accessed=moved, transcendentals=0),
        name=name,
    )
    return lambda ids, *operands: step(ids, *map(in_hbm, operands))
    return lambda ids, *operands: step(ids, *map(in_hbm, operands))


def whole(shape):
    return pl.BlockSpec(shape, lambda i, ids: (0,) * len(shape))


def along(ref, block, width):
    return ref[:, pl.ds(pl.multiple_of(block * width, 128), width)]


def normalise(parts, ids, wanted, gain, strip):
    n, (rows, own) = len(parts), parts[0].shape
    m = len(wanted)

    def kernel(ids_ref, *refs):
        part_refs, (gain_ref, *refs) = refs[:n], refs[n:]
        normed_ref, mean_ref, inv_ref, *out_refs = refs
        total = sum(jnp.sum(r[...].astype(f32), axis=1, keepdims=True) for r in part_refs)
        mean = total * (1.0 / (n * own))
        square = sum(jnp.sum(jnp.square(r[...].astype(f32) - mean), axis=1, keepdims=True) for r in part_refs)
        inv = lax.rsqrt(square * (1.0 / (n * own)) + epsilon)
        mean_ref[...] = jnp.broadcast_to(mean, (strip, 128))
        inv_ref[...] = jnp.broadcast_to(inv, (strip, 128))
        for k in range(n):
            scaled = (part_refs[k][...].astype(f32) - mean) * inv
            normed = (scaled * along(gain_ref, ids_ref[k], own)).astype(bf16)
            normed_ref[:, pl.ds(pl.multiple_of(ids_ref[k] * own, 128), own)] = normed
        for k in range(m):
            out_refs[k][...] = along(normed_ref, ids_ref[n + k], own)

    def strips(width):
        return pl.BlockSpec((strip, width), lambda i, ids: (i, 0))

    return call(
        kernel,
        (rows // strip,),
        [strips(own)] * n + [whole(gain.shape)],
        [strips(n * own)] + [strips(128)] * 2 + [strips(own)] * m,
        [jax.ShapeDtypeStruct((rows, n * own), bf16)]
        + [jax.ShapeDtypeStruct((rows, 128), f32)] * 2
        + [jax.ShapeDtypeStruct((rows, own), bf16)] * m,
        [],
        "normalise",
        10,
        0,
        10 * n * rows * own,
        1,
    )(jnp.stack(ids + wanted), *parts, gain)


def project(normed, w_in, hidden, step):
    rows, width = hidden.shape
    strips = [slice(k * step, (k + 1) * step) for k in range(width // step)]

    def kernel(normed_ref, w_ref, hidden_ref, out_ref, w, done):
        copies = [
            pltpu.make_async_copy(w_ref.at[:, strip], w.at[:, strip], done.at[k]) for k, strip in enumerate(strips)
        ]
        for copy in copies:
            copy.start()
        for copy, strip in zip(copies, strips):
            copy.wait()
            pre = jnp.dot(normed_ref[...], w[:, strip], preferred_element_type=f32)
            out_ref[:, strip] = (hidden_ref[:, strip].astype(f32) * gelu_slope(pre)).astype(bf16)

    return pl.pallas_call(
        kernel,
        grid=(1,),
        in_specs=[
            pl.BlockSpec(normed.shape, lambda j: (0, 0)),
            pl.BlockSpec(memory_space=pl.ANY),
            pl.BlockSpec((rows, width), lambda j: (0, 0)),
        ],
        out_specs=pl.BlockSpec((rows, width), lambda j: (0, 0)),
        out_shape=jax.ShapeDtypeStruct((rows, width), bf16),
        scratch_shapes=[pltpu.VMEM(w_in.shape, bf16), pltpu.SemaphoreType.DMA((len(strips),))],
        compiler_params=pltpu.CompilerParams(vmem_limit_bytes=32 * 2**20),
        cost_estimate=pl.CostEstimate(flops=2 * normed.size * width, bytes_accessed=2 * w_in.size, transcendentals=hidden.size),
        name="project",
    )(normed, in_hbm(w_in), hidden)


def spread(pre_grad, ids, w_in, own, ahead):
    n, (rows, depth) = len(ids), pre_grad.shape

    def kernel(ids_ref, grad_ref, w_ref, *refs):
        out_refs, (blocks, done) = refs[:n], refs[n:]
        copies = [
            pltpu.make_async_copy(
                w_ref.at[pl.ds(pl.multiple_of(ids_ref[k] * own, own), own), :],
                blocks.at[k % ahead],
                done.at[k % ahead],
            )
            for k in range(n)
        ]
        for k in range(ahead):
            copies[k].start()
        for k in range(n):
            copies[k].wait()
            out_refs[k][...] = lax.dot_general(
                grad_ref[...], blocks[k % ahead], (((1,), (1,)), ((), ())), preferred_element_type=f32
            ).astype(bf16)
            if k + ahead < n:
                copies[k + ahead].start()

    return call(
        kernel,
        (1,),
        [whole((rows, depth)), pl.BlockSpec(memory_space=pl.ANY)],
        [whole((rows, own))] * n,
        [jax.ShapeDtypeStruct((rows, own), bf16)] * n,
        [pltpu.VMEM((ahead, own, depth), bf16), pltpu.SemaphoreType.DMA((ahead,))],
        "spread",
        20,
        2 * n * rows * own * depth,
        2 * w_in.size,
    )(jnp.stack(ids), pre_grad, w_in)


def outer(same, crossed, grads, half, width, sides, cores, rows):
    tokens = same[0].shape[0]
    cut = tokens // 2
    terms = [
        [(0, 0, 0, tokens), (1, 0, 1, tokens), (2, 0, 2, tokens), (3, 0, 3, cut), (3, cut, 4, cut)],
        [(0, 0, 0, tokens), (1, 0, 1, tokens), (1, tokens, 3, cut), (2, 0, 2, tokens), (2, tokens, 4, cut)],
    ]

    def kernel(ids_ref, *refs):
        same_refs, crossed_refs, grads_refs, (sent_ref, kept_ref) = refs[:4], refs[4:7], refs[7:12], refs[12:]
        i = pl.program_id(0)
        for side, left_refs in enumerate((same_refs, crossed_refs)):

            @pl.when(ids_ref[i] == side)
            def _():
                column = pl.ds(pl.multiple_of(ids_ref[4 + i] * rows, 128), rows)
                total = None
                for k, at, group, size in terms[side]:
                    term = lax.dot_general(
                        left_refs[k][at : at + size, column],
                        grads_refs[group][...],
                        (((0,), (0,)), ((), ())),
                        preferred_element_type=f32,
                    )
                    total = term if total is None else total + term

                @pl.when(i < 2)
                def _():
                    sent_ref[...] = total.astype(bf16)

                @pl.when(i >= 2)
                def _():
                    kept_ref[...] = total

    return call(
        kernel,
        (4,),
        [whole(p.shape) for p in (*same, *crossed)]
        + [pl.BlockSpec((g.shape[0], width), lambda i, ids: (0, half)) for g in grads],
        [
            pl.BlockSpec((rows, width), lambda i, ids: (jnp.minimum(i, 1), 0)),
            pl.BlockSpec((rows, width), lambda i, ids: (jnp.maximum(i - 2, 0), 0)),
        ],
        [jax.ShapeDtypeStruct((2 * rows, width), bf16), jax.ShapeDtypeStruct((2 * rows, width), f32)],
        [],
        "outer",
        16,
        32 * rows * tokens * width,
        32 * tokens * width,
    )(jnp.stack(sides + cores), *same, *crossed, *grads)


def local(inputs, out_grad, attn_grad, hidden_grad, gain, w_in):
    tokens, own = inputs.shape
    hidden = w_in.shape[1]
    x, zl, c = (lax.axis_index(name) for name in DP)
    zh, y = (lax.axis_index(name) for name in MP)
    gain_row = gain[None, :]
    parity = y % 2
    cut = tokens // 2

    def block(dz, dy):
        return (zh ^ dz) * 4 + (y + dy) % 4

    parts = {(0, 0): inputs}
    parts[1, 0] = shift(inputs, "zh", 1, 2)
    parts[0, 2] = shift(inputs, "y", 2, 4)
    parts[0, 3] = shift(inputs, "y", 1, 4)
    parts[0, 1] = shift(inputs, "y", 3, 4)
    parts[1, 2] = shift(parts[0, 2], "zh", 1, 2)
    parts[1, 3] = shift(parts[1, 0], "y", 1, 4)
    parts[1, 1] = shift(parts[1, 0], "y", 3, 4)
    keys = list(parts)
    wanted = [2 * ((x + step) % 4) + parity for step in range(4)] + [2 * x + 1 - parity]
    normed, mean, inv, *sends, crossed_own = normalise(
        [parts[k] for k in keys], [block(*k) for k in keys], wanted, gain_row, 64
    )

    same = [sends[0], shift(sends[1], "x", 1, 4), shift(sends[3], "x", 3, 4), shift(sends[2], "x", 2, 4)]

    pre_grad = project(normed, w_in, hidden_grad, 512)

    low, high = shift(pre_grad, "x", 1, 4), shift(pre_grad, "x", 3, 4)

    same[3] = after(same[3], pre_grad)
    down = shift(jnp.concatenate([same[1], same[3][:cut]], 0), "y", 3, 4)
    up = shift(jnp.concatenate([same[2], same[3][cut:]], 0), "y", 1, 4)
    crossed = [crossed_own, down, up]

    pieces = dict(zip(keys, spread(pre_grad, [block(*k) for k in keys], w_in, own, 4)))
    got_z = shift(pieces[1, 2], "zh", 1, 2)
    got_p = shift(after(pieces[1, 1], down, up), "y", 1, 4)
    got_m = shift(after(pieces[1, 3], down, up), "y", 3, 4)
    near_p = shift(after(pieces[0, 1], down, up), "y", 1, 4)
    near_m = shift(after(pieces[0, 3], down, up), "y", 3, 4)
    far_sent = (pieces[0, 2].astype(f32) + got_z.astype(f32)).astype(bf16)
    far = shift(far_sent, "y", 2, 4)
    across_sent = (pieces[1, 0].astype(f32) + got_p.astype(f32) + got_m.astype(f32)).astype(bf16)
    across = shift(across_sent, "zh", 1, 2)

    far_low = shift(after(low[:cut], pieces[0, 0]), "x", 1, 4)
    far_high = shift(after(high[cut:], pieces[0, 0]), "x", 3, 4)
    grads = [pre_grad, low, high, far_low, far_high]

    rows = own // 2
    sides = [zl ^ 1 ^ parity, zl ^ parity] * 2
    cores = [1 - c, 1 - c, c, c]
    def pair(value, axis, step, size):
        return value + shift(value, axis, step, size)

    def send_late(kept, got_c):
        late = (kept[:rows] + got_c[:rows].astype(f32)).astype(bf16)
        return late, shift(late, "zl", 1, 2)

    width = hidden // 2
    sent_a, kept_a = outer(same, crossed, [after(pre_grad, far_sent)] + grads[1:], 0, width, sides, cores, rows)
    got_ca = shift(after(sent_a, got_p, got_m), "c", 1, 2)
    ready = after(pre_grad, sent_a)
    sent_b, kept_b = outer(same, crossed, [ready] + grads[1:], 1, width, sides, cores, rows)
    late, got_a = send_late(kept_a, after(got_ca, across, sent_b))
    got_cb = shift(sent_b, "c", 1, 2)
    late, got_b = send_late(kept_b, after(got_cb, got_a))
    weight_a = kept_a[rows:] + got_ca[rows:].astype(f32) + got_a.astype(f32)
    weight_b = kept_b[rows:] + got_cb[rows:].astype(f32) + got_b.astype(f32)
    weight_grad = jnp.concatenate([weight_a, weight_b], 1)

    mean, inv = mean[:, :1], inv[:, :1]
    scaled_own = (inputs.astype(f32) - mean) * inv
    gain_own = lax.dynamic_slice_in_dim(gain, block(0, 0) * own, own, 0)
    dnorm = attn_grad.astype(f32) + pieces[0, 0].astype(f32)
    for value in (near_p, near_m, far, across):
        dnorm = dnorm + value.astype(f32)
    dxhat = dnorm * gain_own
    sums = jnp.stack([jnp.sum(dxhat, axis=1), jnp.sum(dxhat * scaled_own, axis=1)])
    gain_grad = jnp.sum(dnorm * scaled_own, axis=0)

    sums = pair(pair(sums, "y", 2, 4), "zh", 1, 2)
    gain_grad = pair(pair(gain_grad, "c", 1, 2), "zl", 1, 2)
    sums = pair(after(sums, late), "y", 1, 4) * (1.0 / (own * 8))
    gain_grad = pair(pair(after(gain_grad, late), "x", 2, 4), "x", 1, 4)
    first_mean, second_mean = sums[0][:, None], sums[1][:, None]
    input_grad = (out_grad.astype(f32) + inv * (dxhat - first_mean - scaled_own * second_mean)).astype(bf16)
    return (input_grad, weight_grad, gain_grad)


def solution(mesh):
    fine = Mesh(mesh.devices.reshape(4, 2, 2, 2, 4), DP + MP)
    both = P(DP, MP)
    in_specs = (both, both, both, both, P(), P(None, MP))
    out_specs = (both, both, P(MP))
    return jax.shard_map(local, mesh=fine, in_specs=in_specs, out_specs=out_specs, check_vma=False)
```
